256 devices in a mesh: dp: 32 (over z_hi, x, core), tensor: 8 (over z_lo, y).
Axes of the slice: x: 4, y: 4, z: 8 (z_hi: 4, z_lo: 2; z = z_hi * 2 + z_lo), core: 2. Of those that a mesh axis runs over, the one named last changes fastest.
Arguments:
- gate_pre: bfloat16 [16384, 13312], P('dp', 'tensor'), may hold values from -6 to 6
- up_pre: bfloat16 [16384, 13312], P('dp', 'tensor'), may hold values from -6 to 6
- out_grad: bfloat16 [16384, 5120], P('dp', 'tensor'), may hold values from -0.046875 to 0.046875
- master: float32 [5120, 13312], P('dp', 'tensor'), may hold values from -6 to 6
- moment_one: float32 [5120, 13312], P('dp', 'tensor'), may hold values from -3 to 3
- moment_two: float32 [5120, 13312], P('dp', 'tensor'), may hold values from 0.05 to 1
Outputs:
- master_new: float32 [5120, 13312], P('dp', 'tensor')
- moment_one_new: float32 [5120, 13312], P('dp', 'tensor')
- moment_two_new: float32 [5120, 13312], P('dp', 'tensor')
- serving: bfloat16 [5120, 13312], P(('dp', 'tensor'))
The draws below stay inside these ranges and needn't reach their ends.
All inputs are finite; a program needn't handle non-finite values.
Results may differ from the reference program's by a relative error of at most 0.006.
Values may be sent and summed in bfloat16 or wider, within the bound.
No kernel may reach another device: no remote copies, remote signals or barrier semaphores. Data moves between devices by JAX's collectives and lax.ppermute only.
A program may use at most 128 MiB of HBM per device.

```python
import math
import jax
import jax.numpy as jnp
from jax import lax

D = 5120
FF = 13312
TOK_DEV = 512
TOKENS = 16384
N_DP = 32


def spiked(array, rng, source, target, shards_of, factor):
    def block_of(position):
        return (jnp.arange(array.shape[position]) // (array.shape[position] // shards_of)).reshape((-1,) + (1,) * (array.ndim - 1 - position))

    one_side = jax.random.permutation(rng, shards_of)[block_of(target)]
    other_side = (block_of(target) + shards_of // 2) % shards_of
    return jnp.where((block_of(source) == one_side) | (block_of(source) == other_side), factor * array, array)


def block_levels(own_key, dims, pieces, low, high):
    def one(dim, parts):
        heights = jax.random.uniform(jax.random.fold_in(jax.random.fold_in(own_key, 6), dim), (parts,), jnp.float32, low / len(pieces), high / len(pieces))
        return jnp.repeat(jnp.exp(heights), dims[dim] // parts).reshape((-1,) + (1,) * (len(dims) - dim - 1))

    level = one(*pieces[0])
    for cut in pieces[1:]:
        level = level * one(*cut)
    return level


def noise(stream_key, extent, width, limit, shards=(), dtype=jnp.bfloat16):
    drawn = jax.random.normal(stream_key, extent, jnp.float32) * width
    if len(shards) > 0:
        drawn = block_levels(stream_key, extent, shards, -0.22, 0.18) * drawn
    return jnp.clip(drawn, min=-limit, max=limit).astype(dtype)


def noise_with(rng, extent, width, most, pieces, heavy, kind=jnp.bfloat16):
    values = width * jax.random.normal(rng, extent, jnp.float32)
    if pieces:
        values = values * block_levels(rng, extent, pieces, -0.22, 0.18)
    return jnp.clip(spiked(values, jax.random.fold_in(rng, 3), *heavy), -most, most).astype(kind)


def setup_inputs(seed: int = 0) -> dict:
    arg_keys = jax.random.split(jax.random.key(seed), 7)
    gate_pre = noise(arg_keys[0], (TOKENS, FF), 1.0, 6.0, ((0, 32), (1, 8)))
    up_pre = noise(arg_keys[1], (TOKENS, FF), 1.0, 6.0, ((0, 32), (1, 8)))
    out_grad = noise_with(arg_keys[2], (TOKENS, D), (TOKENS ** -0.5), 0.046875, ((0, 32), (1, 8)), (0, 1, 32, 2.75))
    master = noise(arg_keys[3], (D, FF), 1.0, 6.0, ((0, 32), (1, 8)), jnp.float32)
    moment_one = noise(arg_keys[4], (D, FF), 0.5, 3.0, ((0, 32), (1, 8)), jnp.float32)
    moment_two = jnp.clip(jnp.exp(math.log(1.0) - 2.9957323 * jax.random.uniform(arg_keys[5], (D, FF), jnp.float32) ** block_levels(arg_keys[5], (D, FF), ((0, 32), (1, 8)), -0.2, 0.2)), 0.05, 1.0)
    return dict(gate_pre=gate_pre, up_pre=up_pre, out_grad=out_grad, master=master, moment_one=moment_one, moment_two=moment_two)


def reference(gate_pre, up_pre, out_grad, master, moment_one, moment_two):
    hidden = (jax.nn.silu(gate_pre.astype(jnp.float32)) * up_pre.astype(jnp.float32)).astype(jnp.bfloat16)
    hidden_blocks = hidden.reshape(N_DP, TOK_DEV, FF)
    grad_blocks = out_grad.reshape(N_DP, TOK_DEV, D)

    def accumulate(total, pair):
        left, right = pair
        partial_value = jnp.dot(left.astype(jnp.float32).T, right.astype(jnp.float32), precision=lax.Precision.HIGHEST, preferred_element_type=jnp.float32)
        rounded = lax.optimization_barrier(partial_value.astype(jnp.bfloat16))
        return (total + rounded.astype(jnp.float32), None)
    grad, _ = lax.scan(accumulate, jnp.zeros((D, FF), jnp.float32), (grad_blocks, hidden_blocks))
    moment_one_new = 0.9 * moment_one + 0.1 * grad
    moment_two_new = 0.95 * moment_two + 0.05 * grad * grad
    first = moment_one_new / (1.0 - 0.9 ** 20)
    second = moment_two_new / (1.0 - 0.95 ** 20)
    master_new = master - 0.01 * (first / (jnp.sqrt(second) + 1e-08) + 0.1 * master)
    return (master_new, moment_one_new, moment_two_new, master_new.astype(jnp.bfloat16))
```

```python
import jax
import jax.numpy as jnp
import numpy as np
from jax import lax
from jax.experimental import pallas as pl
from jax.experimental.pallas import tpu as pltpu
from jax.sharding import Mesh, PartitionSpec as P

BF = jnp.bfloat16
F32 = jnp.float32
SIZES = {"zh": 4, "x": 4, "c": 2, "zl": 2, "y": 4}
CHUNKS = ((0, 896), (896, 768))


def shift(value, axis, by):
    n = SIZES[axis]
    return lax.ppermute(value, axis, [(i, (i + by) % n) for i in range(n)])


def matmul_kernel(slab_ref, *refs):
    units, tails, pieces = refs[0:7], refs[7:9], refs[9:14]
    out_ref, a_all = refs[14], refs[15]

    @pl.when(pl.program_id(0) == 0)
    def _():
        for u in range(8):
            slab = slab_ref[u]
            for core in range(2):
                row = ((slab // 2) * 4 + core * 2 + slab % 2) * 80
                rows = pl.ds(pl.multiple_of(row, 16), 80)
                for i in range(4):
                    if u < 7:
                        block = units[u][i, core * 80 : core * 80 + 80, :]
                    else:
                        block = tails[i // 2][i % 2, core * 80 : core * 80 + 80, :]
                    a_all[rows, i * 512 : i * 512 + 512] = block

    for m in range(0, 1280, 320):
        total = None
        at = 0
        for piece in pieces:
            depth = piece.shape[0]
            part = jnp.dot(
                a_all[m : m + 320, at : at + depth],
                piece[...],
                preferred_element_type=F32,
            )
            total = part if total is None else total + part
            at += depth
        out_ref[m : m + 320, :] = total.astype(BF)


def matmul(slabs, units, tails, pieces):
    width = pieces[0].shape[1]
    tile = 256
    full = lambda v: pl.BlockSpec(v.shape, lambda j, s: (0,) * v.ndim)
    cols = lambda v: pl.BlockSpec((v.shape[0], tile), lambda j, s: (0, j))
    return pl.pallas_call(
        matmul_kernel,
        grid_spec=pltpu.PrefetchScalarGridSpec(
            num_scalar_prefetch=1,
            grid=(pl.cdiv(width, tile),),
            in_specs=[full(v) for v in units + tails] + [cols(v) for v in pieces],
            out_specs=pl.BlockSpec((1280, tile), lambda j, s: (0, j)),
            scratch_shapes=[pltpu.VMEM((1280, 2048), BF)],
        ),
        out_shape=jax.ShapeDtypeStruct((1280, width), BF),
        compiler_params=pltpu.CompilerParams(vmem_limit_bytes=40 * 2**20),
        cost_estimate=pl.CostEstimate(
            flops=2 * 1280 * 2048 * width,
            bytes_accessed=2 * (1280 * 2048 + 2048 * width + 1280 * width),
            transcendentals=0,
        ),
    )(slabs, *units, *tails, *pieces)


def gather_rows(out_grad):
    x = lax.axis_index("x")
    quarters = out_grad.T.reshape(4, 160, 512)
    pick = lambda by: lax.dynamic_index_in_dim(quarters, (x + by) % 4, 0, keepdims=False)
    own = jnp.stack(
        [pick(0), shift(pick(1), "x", 1), shift(pick(3), "x", -1), shift(pick(2), "x", 2)]
    )
    before = shift(own, "y", 1)
    after = shift(own, "y", -1)
    across = shift(own, "zl", 1)
    opposite = shift(after, "y", -1)
    across_before = shift(across, "y", 1)
    across_after = shift(after, "zl", 1)
    tails = [shift(across_after[:2], "y", -1), shift(across_before[2:], "y", 1)]
    units = [own, before, after, opposite, across, across_before, across_after]
    zl, y = lax.axis_index("zl"), lax.axis_index("y")
    slabs = jnp.stack(
        [
            z * 4 + (y + by) % 4
            for z, steps in ((zl, (0, 3, 1, 2)), (1 - zl, (0, 3, 1, 2)))
            for by in steps
        ]
    ).astype(jnp.int32)
    return slabs, units, tails


def gather_tokens(hidden):
    before = shift(hidden, "x", 1)
    after = shift(hidden, "x", -1)
    return [
        hidden,
        before,
        after,
        shift(before[:256], "x", 1),
        shift(after[256:], "x", -1),
    ]


def on_device(gate_pre, up_pre, out_grad, master, moment_one, moment_two):
    x, c = lax.axis_index("x"), lax.axis_index("c")
    slabs, units, tails = gather_rows(out_grad)
    grads = []
    for start, width in CHUNKS:
        gate = gate_pre[:, start : start + width].astype(F32)
        up = up_pre[:, start : start + width].astype(F32)
        hidden = (jax.nn.silu(gate) * up).astype(BF)
        partial = matmul(slabs, units, tails, gather_tokens(hidden))
        summed = lax.psum_scatter(partial, ("zh", "c"), scatter_dimension=0, tiled=True)
        summed = summed.reshape(2, 80, width)
        first = lax.dynamic_index_in_dim(summed, c, 0, keepdims=False)
        second = lax.dynamic_index_in_dim(summed, 1 - c, 0, keepdims=False)
        devices = [(i, j) for i in range(4) for j in range(2)]
        first = lax.ppermute(
            first, ("x", "c"), [(2 * i + j, 2 * (2 * j + i // 2) + i % 2) for i, j in devices]
        )
        second = lax.ppermute(
            second,
            ("x", "c"),
            [(2 * i + j, 2 * (2 * (1 - j) + i // 2) + i % 2) for i, j in devices],
        )
        low = x < 2
        grads.append(
            jnp.concatenate([jnp.where(low, first, second), jnp.where(low, second, first)], axis=0)
        )
    grad = jnp.concatenate(grads, axis=1).astype(F32)
    moment_one_new = 0.9 * moment_one + 0.1 * grad
    moment_two_new = 0.95 * moment_two + 0.05 * grad * grad
    first = moment_one_new / (1.0 - 0.9**20)
    second = moment_two_new / (1.0 - 0.95**20)
    master_new = master - 0.01 * (first / (jnp.sqrt(second) + 1e-08) + 0.1 * master)
    serving = lax.all_to_all(
        master_new.astype(BF), ("zl", "y"), split_axis=0, concat_axis=1, tiled=True
    )
    return (master_new, moment_one_new, moment_two_new, serving)


def solution(mesh):
    fine = Mesh(mesh.devices.reshape(4, 4, 2, 2, 4), ("zh", "x", "c", "zl", "y"))
    placed = P(("zh", "x", "c"), ("zl", "y"))
    return jax.shard_map(
        on_device,
        mesh=fine,
        in_specs=(placed,) * 6,
        out_specs=(placed, placed, placed, P(("zh", "x", "c", "zl", "y"), None)),
        check_vma=False,
    )
```

```python
import jax
import jax.numpy as jnp
import numpy as np
from jax import lax
from jax.experimental import pallas as pl
from jax.experimental.pallas import tpu as pltpu
from jax.sharding import Mesh, PartitionSpec as P

BF = jnp.bfloat16
F32 = jnp.float32
SIZES = {"zh": 4, "x": 4, "c": 2, "zl": 2, "y": 4}
CHUNKS = ((0, 896), (896, 768))
VMEM_LIMIT = 58 * 2**20


def shift(value, axis, by):
    n = SIZES[axis]
    return lax.ppermute(value, axis, [(i, (i + by) % n) for i in range(n)])


def matmul_kernel(where_ref, *refs):
    slabs, pieces = refs[0:9], refs[9:14]
    keep_ref, send_ref, a_all, b_all, sems = refs[14:19]
    copies = []
    for u, slab in enumerate(slabs):
        tokens = slice(0, 4) if u < 7 else slice(2 * u - 14, 2 * u - 12)
        for core in range(2):
            row = pl.multiple_of(where_ref[2 * min(u, 7) + core], 16)
            copies.append(
                (
                    slab.at[:, pl.ds(core * 80, 80), :],
                    a_all.at[tokens, pl.ds(row, 80), :],
                )
            )
    at = 0
    for piece in pieces:
        copies.append((piece, b_all.at[pl.ds(at, piece.shape[0]), :]))
        at += piece.shape[0]
    copies = [
        pltpu.make_async_copy(source, target, sems.at[n])
        for n, (source, target) in enumerate(copies)
    ]
    for copy in copies:
        copy.start()
    for copy in copies:
        copy.wait()

    width = keep_ref.shape[1]
    for m, out_ref in ((0, keep_ref), (640, send_ref)):
        for n in range(0, width, 512):
            cols = slice(n, min(n + 512, width))
            total = None
            for i in range(4):
                part = jnp.dot(
                    a_all[i, m : m + 640, :],
                    b_all[i * 512 : i * 512 + 512, cols],
                    preferred_element_type=F32,
                )
                total = part if total is None else total + part
            out_ref[:, cols] = total.astype(BF)


def matmul(where, slabs, pieces):
    width = pieces[0].shape[1]
    return pl.pallas_call(
        matmul_kernel,
        in_specs=[pl.BlockSpec(memory_space=pltpu.SMEM)]
        + [pl.BlockSpec(memory_space=pltpu.HBM)] * 14,
        scratch_shapes=[
            pltpu.VMEM((4, 1280, 512), BF),
            pltpu.VMEM((2048, width), BF),
            pltpu.SemaphoreType.DMA((23,)),
        ],
        out_shape=[jax.ShapeDtypeStruct((640, width), BF)] * 2,
        compiler_params=pltpu.CompilerParams(vmem_limit_bytes=VMEM_LIMIT),
        cost_estimate=pl.CostEstimate(flops=1, bytes_accessed=1, transcendentals=0),
    )(where, *slabs, *pieces)


def update_kernel(grad_ref, master_ref, one_ref, two_ref, *refs):
    master_out, one_out, two_out, serving_out = refs[-4:]
    grad = grad_ref[...]
    cols = slice(0, grad.shape[1])
    one = 0.9 * one_ref[:, cols] + 0.1 * grad
    two = 0.95 * two_ref[:, cols] + 0.05 * grad * grad
    first = one / (1.0 - 0.9**20)
    second = two / (1.0 - 0.95**20)
    master = master_ref[:, cols]
    master = master - 0.01 * (first / (jnp.sqrt(second) + 1e-08) + 0.1 * master)
    master_out[:, cols] = master
    one_out[:, cols] = one
    two_out[:, cols] = two
    serving_out[:, cols] = master.astype(BF)


def update(chunk, grad, state, outs):
    width = grad.shape[1]
    block = CHUNKS[0][1]
    wide = pl.BlockSpec((80, block), lambda i: (i, chunk))
    narrow = pl.BlockSpec((80, width), lambda i: (i, 0))
    kept = [pl.BlockSpec(memory_space=pl.ANY)] * len(outs)
    return pl.pallas_call(
        update_kernel,
        grid=(2,),
        in_specs=[narrow, wide, wide, wide] + kept,
        out_specs=[wide] * 4,
        out_shape=[jax.ShapeDtypeStruct(v.shape, F32) for v in state]
        + [jax.ShapeDtypeStruct(state[0].shape, BF)],
        input_output_aliases={4 + i: i for i in range(len(outs))},
        cost_estimate=pl.CostEstimate(flops=1, bytes_accessed=1, transcendentals=0),
    )(grad, *state, *outs)


def gather_rows(quarters):
    x = lax.axis_index("x")
    pick = lambda by: lax.dynamic_index_in_dim(quarters, (x + by) % 4, 0, keepdims=False)
    return jnp.stack(
        [pick(0), shift(pick(1), "x", 1), shift(pick(3), "x", -1), shift(pick(2), "x", 2)]
    )


def slab_rows():
    zh, c, zl, y = (lax.axis_index(name) for name in ("zh", "c", "zl", "y"))
    where = []
    for z in (zl, 1 - zl):
        for by in (0, 3, 1, 2):
            slab = z * 4 + (y + by) % 4
            row = (slab // 2 - zh + 4) % 4 * 160 + slab % 2 * 80
            where += [row + c * 640, row + (1 - c) * 640]
    return jnp.stack(where).astype(jnp.int32)


def to_owner(rows, by):
    c = lax.axis_index("c")
    rows = rows.reshape(2, 80, rows.shape[1])
    sent = []
    for flip in range(2):
        part = lax.dynamic_index_in_dim(rows, (c + flip) % 2, 0, keepdims=False)
        pairs = []
        for z in range(4):
            for i in range(4):
                for j in range(2):
                    owner = ((z + by) % 4 * 4 + 2 * ((j + flip) % 2) + i // 2) * 2 + i % 2
                    pairs.append(((z * 4 + i) * 2 + j, owner))
        sent.append(lax.ppermute(part, ("zh", "x", "c"), pairs))
    return sent


def fold(keep, send):
    return (keep.astype(F32) + shift(send, "c", 1).astype(F32)).astype(BF)


def plus(a, b):
    return (a.astype(F32) + b.astype(F32)).astype(BF)


def tie(*values):
    return lax.optimization_barrier(values)


def ring_first(mine):
    return shift(mine[320:400], "zh", 1), shift(mine[400:480], "zh", -1)


def ring_second(mine, far_up, far_down):
    up = jnp.concatenate([plus(mine[160:240], far_up), mine[240:320]], axis=0)
    down = jnp.concatenate([mine[480:560], plus(mine[560:640], far_down)], axis=0)
    return *to_owner(up, 1), *to_owner(down, -1)


def ring_end(here, up_first, up_second, down_first, down_second):
    total = lambda *values: sum(v.astype(F32) for v in values)
    first = total(here[0], up_first, down_first)
    second = total(here[1], up_second, down_second)
    low = lax.axis_index("x") < 2
    return jnp.concatenate(
        [jnp.where(low, first, second), jnp.where(low, second, first)], axis=0
    )


def on_device(gate_pre, up_pre, out_grad, *state):
    hidden = []
    for start, width in CHUNKS:
        gate = gate_pre[:, start : start + width].astype(F32)
        up = up_pre[:, start : start + width].astype(F32)
        hidden.append((jax.nn.silu(gate) * up).astype(BF))
    own, *hidden = tie(gather_rows(out_grad.T.reshape(4, 160, 512)), *hidden)
    step = lambda v: (shift(v, "x", 1), shift(v, "x", -1))
    last_step = lambda p, n: (shift(p[:256], "x", 1), shift(n[256:], "x", -1))
    prev0, next0 = step(hidden[0])
    before, after, across, prev0, next0 = tie(
        shift(own, "y", 1), shift(own, "y", -1), shift(own, "zl", 1), prev0, next0
    )
    hidden[1], prev0, next0 = tie(hidden[1], prev0, next0)
    far0 = last_step(prev0, next0)
    prev1, next1 = step(hidden[1])
    opposite, across_before, across_after, *far0 = tie(
        shift(after, "y", -1), shift(across, "y", 1), shift(after, "zl", 1), *far0
    )
    tails = [shift(across_after[:2], "y", -1), shift(across_before[2:], "y", 1)]
    slabs = [own, before, after, opposite, across, across_before, across_after, *tails]
    where = slab_rows()
    keep0, send0 = matmul(where, slabs, [hidden[0], prev0, next0, *far0])
    keep0, send0, prev1, next1 = tie(keep0, send0, prev1, next1)
    mine0 = fold(keep0, send0)
    far1 = last_step(prev1, next1)
    rest0 = ring_first(mine0)
    last, *rest0, far1_0, far1_1 = tie(hidden[1], *rest0, *far1)
    rest0 = ring_second(mine0, *rest0)
    keep1, send1 = matmul(where, slabs, [last, prev1, next1, far1_0, far1_1])
    keep1, send1, *rest0 = tie(keep1, send1, *rest0)
    mine1 = fold(keep1, send1)
    far1 = ring_first(mine1)
    here0 = to_owner(mine0[:160], 0)
    here1 = to_owner(mine1[:160], 0)
    far1_up, far1_down, *rest0 = tie(*far1, *rest0)
    outs = update(0, ring_end(here0, *rest0), state, ())
    *rest1, outs0 = tie(*ring_second(mine1, far1_up, far1_down), outs[0])
    outs = update(1, ring_end(here1, *rest1), state, (outs0, *outs[1:]))
    serving = lax.all_to_all(outs[3], ("zl", "y"), split_axis=0, concat_axis=1, tiled=True)
    return (*outs[:3], serving)


def solution(mesh):
    fine = Mesh(mesh.devices.reshape(4, 4, 2, 2, 4), ("zh", "x", "c", "zl", "y"))
    placed = P(("zh", "x", "c"), ("zl", "y"))
    return jax.shard_map(
        on_device,
        mesh=fine,
        in_specs=(placed,) * 6,
        out_specs=(placed, placed, placed, P(("zh", "x", "c", "zl", "y"), None)),
        check_vma=False,
    )
```

```python
import jax
import jax.numpy as jnp
import numpy as np
from jax import lax
from jax.experimental import pallas as pl
from jax.experimental.pallas import tpu as pltpu
from jax.sharding import Mesh, PartitionSpec as P

BF = jnp.bfloat16
F32 = jnp.float32
SIZES = {"zh": 4, "x": 4, "c": 2, "zl": 2, "y": 4}
CHUNKS = ((0, 1024), (1024, 640))
VMEM_LIMIT = 58 * 2**20


def shift(value, axis, by):
    n = SIZES[axis]
    return lax.ppermute(value, axis, [(i, (i + by) % n) for i in range(n)])


def matmul_kernel(where_ref, *refs):
    slabs, pieces = refs[0:9], refs[9:14]
    keep_ref, send_ref, a_all, b_all, sems = refs[14:19]
    copies = []
    for u, slab in enumerate(slabs):
        tokens = slice(0, 4) if u < 7 else slice(2 * u - 14, 2 * u - 12)
        row = pl.multiple_of(where_ref[min(u, 7)], 16)
        copies.append((slab, a_all.at[tokens, pl.ds(row, 160), :]))
    at = 0
    for piece in pieces:
        copies.append((piece, b_all.at[pl.ds(at, piece.shape[0]), :]))
        at += piece.shape[0]
    copies = [
        pltpu.make_async_copy(source, target, sems.at[n])
        for n, (source, target) in enumerate(copies)
    ]
    for copy in copies:
        copy.start()
    for copy in copies:
        copy.wait()

    width = keep_ref.shape[1]
    for m, out_ref in ((0, keep_ref), (640, send_ref)):
        for n in range(0, width, 512):
            cols = slice(n, min(n + 512, width))
            total = None
            for i in range(4):
                part = jnp.dot(
                    a_all[i, m : m + 640, :],
                    b_all[i * 512 : i * 512 + 512, cols],
                    preferred_element_type=F32,
                )
                total = part if total is None else total + part
            out_ref[:, cols] = total.astype(BF)


def matmul(where, slabs, pieces):
    width = pieces[0].shape[1]
    return pl.pallas_call(
        matmul_kernel,
        in_specs=[pl.BlockSpec(memory_space=pltpu.SMEM)]
        + [pl.BlockSpec(memory_space=pltpu.HBM)] * 14,
        scratch_shapes=[
            pltpu.VMEM((4, 1280, 512), BF),
            pltpu.VMEM((2048, width), BF),
            pltpu.SemaphoreType.DMA((14,)),
        ],
        out_shape=[jax.ShapeDtypeStruct((640, width), BF)] * 2,
        compiler_params=pltpu.CompilerParams(vmem_limit_bytes=VMEM_LIMIT),
        cost_estimate=pl.CostEstimate(flops=1, bytes_accessed=1, transcendentals=0),
    )(where, *slabs, *pieces)


def gather_rows(quarters):
    x = lax.axis_index("x")
    pick = lambda by: lax.dynamic_index_in_dim(quarters, (x + by) % 4, 0, keepdims=False)
    return jnp.stack(
        [pick(0), shift(pick(1), "x", 1), shift(pick(3), "x", -1), shift(pick(2), "x", 2)]
    )


def slab_rows():
    zh, c, zl, y = (lax.axis_index(name) for name in ("zh", "c", "zl", "y"))
    where = []
    for z in (zl, 1 - zl):
        for by in (0, 3, 1, 2):
            slab = z * 4 + (y + by) % 4
            where.append((slab // 2 - zh + 4) % 4 * 160 + (slab + c) % 2 * 640)
    return jnp.stack(where).astype(jnp.int32)


def to_owner(rows, by):
    pairs = []
    for z in range(4):
        for i in range(4):
            for j in range(2):
                owner = ((z + by) % 4 * 4 + 2 * j + i // 2) * 2 + i % 2
                pairs.append(((z * 4 + i) * 2 + j, owner))
    return lax.ppermute(rows, ("zh", "x", "c"), pairs)


@jax.named_scope("core_sum")
def fold(keep, send):
    return (keep.astype(F32) + shift(send, "c", 1).astype(F32)).astype(BF)


def plus(a, b):
    return (a.astype(F32) + b.astype(F32)).astype(BF)


def tie(*values):
    return lax.optimization_barrier(values)


@jax.named_scope("relay")
def ring_first(mine):
    return shift(mine[320:400], "zh", 1), shift(mine[400:480], "zh", -1)


@jax.named_scope("to_owner")
def ring_second(mine, far_up, far_down):
    up = jnp.concatenate([plus(mine[160:240], far_up), mine[240:320]], axis=0)
    down = jnp.concatenate([mine[480:560], plus(mine[560:640], far_down)], axis=0)
    return to_owner(up, 1), to_owner(down, -1)


@jax.named_scope("own_to_owner")
def ring_here(mine):
    return to_owner(mine, 0)


def on_device(gate_pre, up_pre, out_grad, master, moment_one, moment_two):
    hidden = []
    for start, width in CHUNKS:
        gate = gate_pre[:, start : start + width].astype(F32)
        up = up_pre[:, start : start + width].astype(F32)
        hidden.append((jax.nn.silu(gate) * up).astype(BF))
    own, *hidden = tie(gather_rows(out_grad.T.reshape(4, 160, 512)), *hidden)
    step = lambda v: (shift(v, "x", 1), shift(v, "x", -1))
    last_step = lambda p, n: (shift(p[:256], "x", 1), shift(n[256:], "x", -1))
    prev0, next0 = step(hidden[0])
    before, after, across, prev0, next0 = tie(
        shift(own, "y", 1), shift(own, "y", -1), shift(own, "zl", 1), prev0, next0
    )
    hidden[1], prev0, next0 = tie(hidden[1], prev0, next0)
    far0 = last_step(prev0, next0)
    prev1, next1 = step(hidden[1])
    opposite, across_before, across_after, *far0 = tie(
        shift(after, "y", -1), shift(across, "y", 1), shift(after, "zl", 1), *far0
    )
    tails = [shift(across_after[:2], "y", -1), shift(across_before[2:], "y", 1)]
    slabs = [own, before, after, opposite, across, across_before, across_after, *tails]
    where = slab_rows()
    keep0, send0 = matmul(where, slabs, [hidden[0], prev0, next0, *far0])
    far1 = last_step(prev1, next1)
    keep0, send0, *far1 = tie(keep0, send0, *far1)
    mine0 = fold(keep0, send0)
    relay0 = ring_first(mine0)
    keep1, send1 = matmul(where, slabs, [hidden[1], prev1, next1, *far1])
    keep1, send1, *relay0 = tie(keep1, send1, *relay0)
    rest0 = ring_second(mine0, *relay0)
    here0, relay0 = tie(mine0[:160], relay0[0])
    here0 = ring_here(here0)
    mine1 = fold(keep1, send1)
    relay1 = ring_first(mine1)
    up1, down1, here1, *rest0 = tie(*relay1, mine1[:160], *rest0)
    here1 = ring_here(here1)
    rest1 = ring_second(mine1, up1, down1)

    total = lambda *values: sum(v.astype(F32) for v in values)
    grad = jnp.concatenate([total(here0, *rest0), total(here1, *rest1)], axis=1)
    moment_one_new = 0.9 * moment_one + 0.1 * grad
    moment_two_new = 0.95 * moment_two + 0.05 * grad * grad
    first = moment_one_new / (1.0 - 0.9**20)
    second = moment_two_new / (1.0 - 0.95**20)
    master_new = master - 0.01 * (first / (jnp.sqrt(second) + 1e-08) + 0.1 * master)
    serving = lax.all_to_all(
        master_new.astype(BF), ("zl", "y"), split_axis=0, concat_axis=1, tiled=True
    )
    return (master_new, moment_one_new, moment_two_new, serving)


def solution(mesh):
    fine = Mesh(mesh.devices.reshape(4, 4, 2, 2, 4), ("zh", "x", "c", "zl", "y"))
    placed = P(("zh", "x", "c"), ("zl", "y"))
    return jax.shard_map(
        on_device,
        mesh=fine,
        in_specs=(placed,) * 6,
        out_specs=(placed, placed, placed, P(("zh", "x", "c", "zl", "y"), None)),
        check_vma=False,
    )
```

```python
import jax
import jax.numpy as jnp
import numpy as np
from jax import lax
from jax.experimental import pallas as pl
from jax.experimental.pallas import tpu as pltpu
from jax.sharding import Mesh, PartitionSpec as P

BF = jnp.bfloat16
F32 = jnp.float32
SIZES = {"zh": 4, "x": 4, "c": 2, "zl": 2, "y": 4}
CHUNKS = ((0, 1024), (1024, 640))
VMEM_LIMIT = 58 * 2**20


def shift(value, axis, by):
    n = SIZES[axis]
    return lax.ppermute(value, axis, [(i, (i + by) % n) for i in range(n)])


def start(copies, sems, first):
    copies = [
        pltpu.make_async_copy(source, target, sems.at[first + n])
        for n, (source, target) in enumerate(copies)
    ]
    for copy in copies:
        copy.start()
    return copies


def wait(copies):
    for copy in copies:
        copy.wait()


def matmul_kernel(where_ref, *refs):
    slabs, pieces = refs[0:9], refs[9:14]
    keep_ref, send_ref, a_all, b_all, sems = refs[14:19]
    width = keep_ref.shape[1]
    tiles = [pl.ds(n, min(512, width - n)) for n in range(0, width, 512)]
    loads = []
    for number, group in enumerate(((0, 3, 4, 7, 8), (1, 2, 5, 6))):
        copies = []
        for u in group:
            row = pl.multiple_of(where_ref[min(u, 7)], 16) + 640 * number
            tokens = slice(0, 4) if u < 7 else slice(2 * u - 14, 2 * u - 12)
            copies.append((slabs[u], a_all.at[tokens, pl.ds(row, 160), :]))
        loads.append(copies)
    for n, cols in enumerate(tiles):
        copies, at = [], 0
        for piece in pieces:
            copies.append((piece.at[:, cols], b_all.at[pl.ds(at, piece.shape[0]), cols]))
            at += piece.shape[0]
        loads.insert(1 + n, copies)
    pending, first = [], 0
    for copies in loads:
        pending.append(start(copies, sems, first))
        first += len(copies)

    def product(rows, out_ref, cols):
        total = None
        for i in range(4):
            part = jnp.dot(
                a_all[i, rows, :],
                b_all[i * 512 : i * 512 + 512, cols],
                preferred_element_type=F32,
            )
            total = part if total is None else total + part
        out_ref[:, cols] = total.astype(BF)

    def both(first_ref, second_ref):
        wait(pending[0])
        for copies, cols in zip(pending[1:-1], tiles):
            wait(copies)
            product(slice(0, 640), first_ref, cols)
        wait(pending[-1])
        for cols in tiles:
            product(slice(640, 1280), second_ref, cols)

    kept = where_ref[8] == 0

    @pl.when(kept)
    def _():
        both(keep_ref, send_ref)

    @pl.when(jnp.logical_not(kept))
    def _():
        both(send_ref, keep_ref)


def matmul(where, slabs, pieces):
    width = pieces[0].shape[1]
    return pl.pallas_call(
        matmul_kernel,
        in_specs=[pl.BlockSpec(memory_space=pltpu.SMEM)]
        + [pl.BlockSpec(memory_space=pltpu.HBM)] * 14,
        scratch_shapes=[
            pltpu.VMEM((4, 1280, 512), BF),
            pltpu.VMEM((2048, width), BF),
            pltpu.SemaphoreType.DMA((9 + 5 * pl.cdiv(width, 512),)),
        ],
        out_shape=[jax.ShapeDtypeStruct((640, width), BF)] * 2,
        compiler_params=pltpu.CompilerParams(vmem_limit_bytes=VMEM_LIMIT),
        cost_estimate=pl.CostEstimate(flops=1, bytes_accessed=1, transcendentals=0),
    )(where, *slabs, *pieces)


def gather_rows(quarters):
    x = lax.axis_index("x")
    pick = lambda by: lax.dynamic_index_in_dim(quarters, (x + by) % 4, 0, keepdims=False)
    return jnp.stack(
        [pick(0), shift(pick(1), "x", 1), shift(pick(3), "x", -1), shift(pick(2), "x", 2)]
    )


def slab_rows():
    zh, c, zl, y = (lax.axis_index(name) for name in ("zh", "c", "zl", "y"))
    where = []
    for z in (zl, 1 - zl):
        for by in (0, 3, 1, 2):
            slab = z * 4 + (y + by) % 4
            where.append((slab // 2 - zh + 4) % 4 * 160)
    where.append((y + c) % 2)
    return jnp.stack(where).astype(jnp.int32)


def to_owner(rows, by):
    pairs = []
    for z in range(4):
        for i in range(4):
            for j in range(2):
                owner = ((z + by) % 4 * 4 + 2 * j + i // 2) * 2 + i % 2
                pairs.append(((z * 4 + i) * 2 + j, owner))
    return lax.ppermute(rows, ("zh", "x", "c"), pairs)


def plus(*values):
    return sum(v.astype(F32) for v in values).astype(BF)


def tie(*values):
    return lax.optimization_barrier(values)


@jax.named_scope("relay")
def ring_first(keep, got):
    far = plus(keep[320:480], got[320:480])
    return shift(far[:80], "zh", 1), shift(far[80:], "zh", -1)


@jax.named_scope("to_owner")
def ring_second(keep, got, far_up, far_down):
    part = lambda a, b, *more: plus(keep[a:b], got[a:b], *more)
    up = jnp.concatenate([part(160, 240, far_up), part(240, 320)], axis=0)
    down = jnp.concatenate([part(480, 560), part(560, 640, far_down)], axis=0)
    return to_owner(up, 1), to_owner(down, -1)


@jax.named_scope("own_to_owner")
def ring_here(keep, got):
    return to_owner(plus(keep[:160], got[:160]), 0)


def on_device(gate_pre, up_pre, out_grad, master, moment_one, moment_two):
    hidden = []
    for start, width in CHUNKS:
        gate = gate_pre[:, start : start + width].astype(F32)
        up = up_pre[:, start : start + width].astype(F32)
        hidden.append((jax.nn.silu(gate) * up).astype(BF))
    own, *hidden = tie(gather_rows(out_grad.T.reshape(4, 160, 512)), *hidden)
    step = lambda v: (shift(v, "x", 1), shift(v, "x", -1))
    last_step = lambda p, n: (shift(p[:256], "x", 1), shift(n[256:], "x", -1))
    prev0, next0 = step(hidden[0])
    before, after, across, prev0, next0 = tie(
        shift(own, "y", 1), shift(own, "y", -1), shift(own, "zl", 1), prev0, next0
    )
    hidden[1], prev0, next0 = tie(hidden[1], prev0, next0)
    far0 = last_step(prev0, next0)
    prev1, next1 = step(hidden[1])
    opposite, across_before, across_after, *far0 = tie(
        shift(after, "y", -1), shift(across, "y", 1), shift(after, "zl", 1), *far0
    )
    tails = [shift(across_after[:2], "y", -1), shift(across_before[2:], "y", 1)]
    slabs = [own, before, after, opposite, across, across_before, across_after, *tails]
    where = slab_rows()
    keep0, send0 = matmul(where, slabs, [hidden[0], prev0, next0, *far0])
    far1 = last_step(prev1, next1)
    keep0, send0, *far1 = tie(keep0, send0, *far1)
    got0 = shift(send0, "c", 1)
    relay0 = ring_first(keep0, got0)
    keep1, send1 = matmul(where, slabs, [hidden[1], prev1, next1, *far1])
    keep1, send1, *relay0 = tie(keep1, send1, *relay0)
    rest0 = ring_second(keep0, got0, *relay0)
    here0, relay0 = tie(keep0, relay0[0])
    here0 = ring_here(here0, got0)
    got1 = shift(send1, "c", 1)
    relay1 = ring_first(keep1, got1)
    up1, down1, *rest0 = tie(*relay1, *rest0)
    rest1 = ring_second(keep1, got1, up1, down1)
    here1 = ring_here(keep1, got1)
    here0, here1, *rest1 = tie(here0, here1, *rest1)

    total = lambda *values: sum(v.astype(F32) for v in values)
    grad = jnp.concatenate([total(here0, *rest0), total(here1, *rest1)], axis=1)
    moment_one_new = 0.9 * moment_one + 0.1 * grad
    moment_two_new = 0.95 * moment_two + 0.05 * grad * grad
    first = moment_one_new / (1.0 - 0.9**20)
    second = moment_two_new / (1.0 - 0.95**20)
    master_new = master - 0.01 * (first / (jnp.sqrt(second) + 1e-08) + 0.1 * master)
    serving = lax.all_to_all(
        master_new.astype(BF), ("zl", "y"), split_axis=0, concat_axis=1, tiled=True
    )
    return (master_new, moment_one_new, moment_two_new, serving)


def solution(mesh):
    fine = Mesh(mesh.devices.reshape(4, 4, 2, 2, 4), ("zh", "x", "c", "zl", "y"))
    placed = P(("zh", "x", "c"), ("zl", "y"))
    return jax.shard_map(
        on_device,
        mesh=fine,
        in_specs=(placed,) * 6,
        out_specs=(placed, placed, placed, P(("zh", "x", "c", "zl", "y"), None)),
        check_vma=False,
    )
```

```python
import jax
import jax.numpy as jnp
import numpy as np
from jax import lax
from jax.experimental import pallas as pl
from jax.experimental.pallas import tpu as pltpu
from jax.sharding import Mesh, PartitionSpec as P

BF = jnp.bfloat16
F32 = jnp.float32
SIZES = {"zh": 4, "x": 4, "c": 2, "zl": 2, "y": 4}
CHUNKS = ((0, 1024), (1024, 640))
VMEM_LIMIT = 58 * 2**20


def shift(value, axis, by):
    n = SIZES[axis]
    return lax.ppermute(value, axis, [(i, (i + by) % n) for i in range(n)])


def matmul_kernel(where_ref, *refs):
    slabs, pieces = refs[0:9], refs[9:14]
    keep_ref, send_ref, a_all, b_all, sems = refs[14:19]
    copies = []
    for u, slab in enumerate(slabs):
        tokens = slice(0, 4) if u < 7 else slice(2 * u - 14, 2 * u - 12)
        row = pl.multiple_of(where_ref[min(u, 7)], 16)
        copies.append((slab, a_all.at[tokens, pl.ds(row, 160), :]))
    at = 0
    for piece in pieces:
        copies.append((piece, b_all.at[pl.ds(at, piece.shape[0]), :]))
        at += piece.shape[0]
    copies = [
        pltpu.make_async_copy(source, target, sems.at[n])
        for n, (source, target) in enumerate(copies)
    ]
    for copy in copies:
        copy.start()
    for copy in copies:
        copy.wait()

    width = keep_ref.shape[1]
    for m, out_ref in ((0, keep_ref), (640, send_ref)):
        for n in range(0, width, 512):
            cols = slice(n, min(n + 512, width))
            total = None
            for i in range(4):
                part = jnp.dot(
                    a_all[i, m : m + 640, :],
                    b_all[i * 512 : i * 512 + 512, cols],
                    preferred_element_type=F32,
                )
                total = part if total is None else total + part
            out_ref[:, cols] = total.astype(BF)


def matmul(where, slabs, pieces):
    width = pieces[0].shape[1]
    return pl.pallas_call(
        matmul_kernel,
        in_specs=[pl.BlockSpec(memory_space=pltpu.SMEM)]
        + [pl.BlockSpec(memory_space=pltpu.HBM)] * 14,
        scratch_shapes=[
            pltpu.VMEM((4, 1280, 512), BF),
            pltpu.VMEM((2048, width), BF),
            pltpu.SemaphoreType.DMA((14,)),
        ],
        out_shape=[jax.ShapeDtypeStruct((640, width), BF)] * 2,
        compiler_params=pltpu.CompilerParams(vmem_limit_bytes=VMEM_LIMIT),
        cost_estimate=pl.CostEstimate(flops=1, bytes_accessed=1, transcendentals=0),
    )(where, *slabs, *pieces)


def gather_rows(quarters):
    x = lax.axis_index("x")
    pick = lambda by: lax.dynamic_index_in_dim(quarters, (x + by) % 4, 0, keepdims=False)
    return jnp.stack(
        [pick(0), shift(pick(1), "x", 1), shift(pick(3), "x", -1), shift(pick(2), "x", 2)]
    )


def slab_rows():
    zh, c, zl, y = (lax.axis_index(name) for name in ("zh", "c", "zl", "y"))
    where = []
    for z in (zl, 1 - zl):
        for by in (0, 3, 1, 2):
            slab = z * 4 + (y + by) % 4
            where.append((slab // 2 - zh + 4) % 4 * 160 + (slab + c) % 2 * 640)
    return jnp.stack(where).astype(jnp.int32)


def to_owner(rows, by):
    pairs = []
    for z in range(4):
        for i in range(4):
            for j in range(2):
                owner = ((z + by) % 4 * 4 + 2 * j + i // 2) * 2 + i % 2
                pairs.append(((z * 4 + i) * 2 + j, owner))
    return lax.ppermute(rows, ("zh", "x", "c"), pairs)


@jax.named_scope("core_sum")
def fold(keep, send):
    return (keep.astype(F32) + shift(send, "c", 1).astype(F32)).astype(BF)


def plus(a, b):
    return (a.astype(F32) + b.astype(F32)).astype(BF)


def tie(*values):
    return lax.optimization_barrier(values)


@jax.named_scope("relay")
def ring_first(mine):
    return shift(mine[320:400], "zh", 1), shift(mine[400:480], "zh", -1)


@jax.named_scope("to_owner")
def ring_second(mine, far_up, far_down):
    up = jnp.concatenate([plus(mine[160:240], far_up), mine[240:320]], axis=0)
    down = jnp.concatenate([mine[480:560], plus(mine[560:640], far_down)], axis=0)
    return to_owner(up, 1), to_owner(down, -1)


@jax.named_scope("own_to_owner")
def ring_here(mine):
    return to_owner(mine, 0)


def on_device(gate_pre, up_pre, out_grad, master, moment_one, moment_two):
    hidden = []
    for start, width in CHUNKS:
        gate = gate_pre[:, start : start + width].astype(F32)
        up = up_pre[:, start : start + width].astype(F32)
        hidden.append((jax.nn.silu(gate) * up).astype(BF))
    own, *hidden = tie(gather_rows(out_grad.T.reshape(4, 160, 512)), *hidden)
    step = lambda v: (shift(v, "x", 1), shift(v, "x", -1))
    last_step = lambda p, n: (shift(p[:256], "x", 1), shift(n[256:], "x", -1))
    prev0, next0 = step(hidden[0])
    before, after, across, prev0, next0 = tie(
        shift(own, "y", 1), shift(own, "y", -1), shift(own, "zl", 1), prev0, next0
    )
    hidden[1], prev0, next0 = tie(hidden[1], prev0, next0)
    far0 = last_step(prev0, next0)
    prev1, next1 = step(hidden[1])
    opposite, across_before, across_after, *far0 = tie(
        shift(after, "y", -1), shift(across, "y", 1), shift(after, "zl", 1), *far0
    )
    tails = [shift(across_after[:2], "y", -1), shift(across_before[2:], "y", 1)]
    slabs = [own, before, after, opposite, across, across_before, across_after, *tails]
    where = slab_rows()
    keep0, send0 = matmul(where, slabs, [hidden[0], prev0, next0, *far0])
    far1 = last_step(prev1, next1)
    keep0, send0, *far1 = tie(keep0, send0, *far1)
    mine0 = fold(keep0, send0)
    relay0 = ring_first(mine0)
    keep1, send1 = matmul(where, slabs, [hidden[1], prev1, next1, *far1])
    keep1, send1, *relay0 = tie(keep1, send1, *relay0)
    rest0 = ring_second(mine0, *relay0)
    here0, relay0 = tie(mine0[:160], relay0[0])
    here0 = ring_here(here0)
    mine1 = fold(keep1, send1)
    relay1 = ring_first(mine1)
    up1, down1, here1, *rest0 = tie(*relay1, mine1[:160], *rest0)
    here1 = ring_here(here1)
    rest1 = ring_second(mine1, up1, down1)

    total = lambda *values: sum(v.astype(F32) for v in values)

    def adamw(parts):
        grad = jnp.concatenate([total(*parts[:3]), total(*parts[3:])], axis=1)
        moment_one_new = 0.9 * moment_one + 0.1 * grad
        moment_two_new = 0.95 * moment_two + 0.05 * grad * grad
        first = moment_one_new / (1.0 - 0.9**20)
        second = moment_two_new / (1.0 - 0.95**20)
        master_new = master - 0.01 * (first / (jnp.sqrt(second) + 1e-08) + 0.1 * master)
        return master_new, moment_one_new, moment_two_new

    parts = [here0, *rest0, here1, *rest1]
    rows, *parts = tie(adamw(parts)[0].astype(BF), *parts)
    serving = lax.all_to_all(rows, ("zl", "y"), split_axis=0, concat_axis=1, tiled=True)
    return (*adamw(parts), serving)


def solution(mesh):
    fine = Mesh(mesh.devices.reshape(4, 4, 2, 2, 4), ("zh", "x", "c", "zl", "y"))
    placed = P(("zh", "x", "c"), ("zl", "y"))
    return jax.shard_map(
        on_device,
        mesh=fine,
        in_specs=(placed,) * 6,
        out_specs=(placed, placed, placed, P(("zh", "x", "c", "zl", "y"), None)),
        check_vma=False,
    )
```
